128 devices in a mesh: row: 16 (over x, y), col: 8 (over z, core).
Axes of the slice: x: 4, y: 4, z: 4, core: 2. Of those that a mesh axis runs over, the one named last changes fastest.
Arguments:
- x_codes: int32 [1024, 8192], P('row', 'col'), may hold values from -127 to 127, as said below
- x_exp: int32 [8192], P('col'), may hold values from -8 to -6
- gate_codes: int32 [8192, 14336], P('col', 'row'), may hold values from -8 to 7
- gate_exp: int32 [14336], P('row'), may hold values from -8 to -6
- up_codes: int32 [8192, 14336], P('col', 'row'), may hold values from -8 to 7
- up_exp: int32 [14336], P('row'), may hold values from -8 to -6
- down_codes: int32 [14336, 8192], P('row', 'col'), may hold values from -8 to 7
- down_exp: int32 [8192], P('col'), may hold values from -10 to -8
- target: bfloat16 [1024, 8192], P('row', 'col'), may hold values from -6 to 6
Outputs:
- grad_x: float32 [1024, 8192], P('row', 'col')
- grad_gate: float32 [8192, 14336], P('col', 'row')
- grad_up: float32 [8192, 14336], P('col', 'row')
- grad_down: float32 [14336, 8192], P('row', 'col')
- gate_exp_grad: float32 [14336], P('row')
- up_exp_grad: float32 [14336], P('row')
- down_exp_grad: float32 [8192], P('col')
The draws below stay inside these ranges and needn't reach their ends.
Inputs may be any that keep to these rules, and one draw needn't show every extreme that they name: `x_codes`: activation codes; many sit at the clip values.
All inputs are finite; a program needn't handle non-finite values.
Results may differ from the reference program's by a relative error of at most 0.0033.
Values may be sent and summed in bfloat16 or wider, within the bound.
A program may use at most 128 MiB of HBM per device.

```python
import math
import jax
import jax.numpy as jnp

D = 8192
F = 14336
TOKENS = 1024


def draw_x_codes(key, part):
    key = jax.random.fold_in(key, 11)
    raw = jax.random.randint(key, (TOKENS, D), -180, 181)
    return jnp.clip(raw, -127, 127).astype(jnp.int32)


def plant(entries, rng, least, high):
    longest = entries.shape.index(max(entries.shape))
    spots = []
    for shift in (0, 1):
        where = [jax.random.randint(jax.random.fold_in(rng, axis), (), 0, length) for axis, length in enumerate(entries.shape)]
        where[longest] = (where[longest] + shift) % entries.shape[longest]
        spots.append(tuple(where))
    return entries.at[spots[0]].set(least).at[spots[1]].set(high)


def levels(own_key, extent, cuts, low, top_value):
    loudness = 1.0
    for position, parts in cuts:
        draws = jax.random.uniform(jax.random.fold_in(jax.random.fold_in(own_key, 6), position), (parts,), jnp.float32, low / len(cuts), top_value / len(cuts))
        loudness = loudness * jnp.repeat(jnp.exp(draws), extent[position] // parts).reshape((-1,) + (1,) * (len(extent) - 1 - position))
    return loudness


def scatter_about(key, extent, spread, most, shards=(), dtype=jnp.bfloat16):
    entries = jax.random.normal(key, extent, jnp.float32) * spread
    if len(shards) > 0:
        entries = levels(key, extent, shards, -0.22, 0.18) * entries
    return jnp.clip(entries, min=-most, max=most).astype(dtype)


def setup_inputs(seed: int = 0) -> dict:
    keys = jax.random.split(jax.random.key(seed), 10)
    x_codes = draw_x_codes(jax.random.fold_in(keys[9], 71), 0)
    x_exp = plant(jax.random.randint(keys[1], (D,), -8, -5), jax.random.fold_in(keys[1], 1), -8, (-5) - 1).astype(jnp.int32)
    gate_codes = plant(jax.random.randint(keys[2], (D, F), -8, 8), jax.random.fold_in(keys[2], 1), -8, 7).astype(jnp.int32)
    gate_exp = plant(jax.random.randint(keys[3], (F,), -5 - min(1, D // 256) - min(1, D // 1024) - min(1, D // 4096), -2 - min(1, D // 256) - min(1, D // 1024) - min(1, D // 4096)), jax.random.fold_in(keys[3], 1), -5 - min(1, D // 256) - min(1, D // 1024) - min(1, D // 4096), (-2 - min(1, D // 256) - min(1, D // 1024) - min(1, D // 4096)) - 1).astype(jnp.int32)
    up_codes = plant(jax.random.randint(keys[4], (D, F), -8, 8), jax.random.fold_in(keys[4], 1), -8, 7).astype(jnp.int32)
    up_exp = plant(jax.random.randint(keys[5], (F,), -5 - min(1, D // 256) - min(1, D // 1024) - min(1, D // 4096), -2 - min(1, D // 256) - min(1, D // 1024) - min(1, D // 4096)), jax.random.fold_in(keys[5], 1), -5 - min(1, D // 256) - min(1, D // 1024) - min(1, D // 4096), (-2 - min(1, D // 256) - min(1, D // 1024) - min(1, D // 4096)) - 1).astype(jnp.int32)
    down_codes = plant(jax.random.randint(keys[6], (F, D), -8, 8), jax.random.fold_in(keys[6], 1), -8, 7).astype(jnp.int32)
    down_exp = plant(jax.random.randint(keys[7], (D,), -7 - min(1, F // 256) - min(1, F // 1024) - min(1, F // 4096), -4 - min(1, F // 256) - min(1, F // 1024) - min(1, F // 4096)), jax.random.fold_in(keys[7], 1), -7 - min(1, F // 256) - min(1, F // 1024) - min(1, F // 4096), (-4 - min(1, F // 256) - min(1, F // 1024) - min(1, F // 4096)) - 1).astype(jnp.int32)
    target = scatter_about(keys[8], (TOKENS, D), 1.0, 6.0, ((0, 16), (1, 8)))
    return {"x_codes": x_codes, "x_exp": x_exp, "gate_codes": gate_codes, "gate_exp": gate_exp, "up_codes": up_codes, "up_exp": up_exp, "down_codes": down_codes, "down_exp": down_exp, "target": target}


log_two = math.log(2.0)


def power_two(exponent):
    return jnp.exp2(exponent.astype(jnp.float32))


def dequant(codes, exponent):
    return (codes.astype(jnp.float32) * power_two(exponent)[None, :]).astype(jnp.bfloat16)


def inside(codes):
    return jnp.logical_and(codes > -8, codes < 7)


def reference(x_codes, x_exp, gate_codes, gate_exp, up_codes, up_exp, down_codes, down_exp, target):
    x_value = dequant(x_codes, x_exp)
    w_gate = dequant(gate_codes, gate_exp)
    w_up = dequant(up_codes, up_exp)
    w_down = dequant(down_codes, down_exp)
    gate_sum = jnp.dot(x_value, w_gate, preferred_element_type=jnp.float32)
    up_sum = jnp.dot(x_value, w_up, preferred_element_type=jnp.float32)
    logistic = jax.nn.sigmoid(gate_sum)
    activated = gate_sum * logistic
    hidden = (activated * up_sum).astype(jnp.bfloat16)
    output_sum = jnp.dot(hidden, w_down, preferred_element_type=jnp.float32)
    delta = (output_sum - target.astype(jnp.float32)).astype(jnp.bfloat16)
    back_sum = jnp.dot(delta, w_down.T, preferred_element_type=jnp.float32)
    up_delta = (back_sum * activated).astype(jnp.bfloat16)
    gate_delta = (back_sum * up_sum * logistic * (1.0 + gate_sum * (1.0 - logistic))).astype(jnp.bfloat16)
    gate_full = jnp.dot(x_value.T, gate_delta, preferred_element_type=jnp.float32)
    up_full = jnp.dot(x_value.T, up_delta, preferred_element_type=jnp.float32)
    down_full = jnp.dot(hidden.T, delta, preferred_element_type=jnp.float32)
    input_sum = jnp.dot(gate_delta, w_gate.T, preferred_element_type=jnp.float32) + jnp.dot(up_delta, w_up.T, preferred_element_type=jnp.float32)
    grad_x = jnp.where(jnp.abs(x_codes) < 127, input_sum, jnp.float32(0.0))
    grad_gate = jnp.where(inside(gate_codes), gate_full, jnp.float32(0.0))
    grad_up = jnp.where(inside(up_codes), up_full, jnp.float32(0.0))
    grad_down = jnp.where(inside(down_codes), down_full, jnp.float32(0.0))
    gate_exp_grad = log_two * power_two(gate_exp) * jnp.sum(gate_full * gate_codes.astype(jnp.float32), axis=0)
    up_exp_grad = log_two * power_two(up_exp) * jnp.sum(up_full * up_codes.astype(jnp.float32), axis=0)
    down_exp_grad = log_two * power_two(down_exp) * jnp.sum(down_full * down_codes.astype(jnp.float32), axis=0)
    return (grad_x, grad_gate, grad_up, grad_down, gate_exp_grad, up_exp_grad, down_exp_grad)
```

```python
import math

import jax
import jax.numpy as jnp
from jax import lax
from jax.experimental import pallas as pl
from jax.experimental.pallas import tpu as pltpu
from jax.sharding import PartitionSpec as P

LN2 = math.log(2.0)
F32, BF16 = jnp.float32, jnp.bfloat16
NN = (((1,), (0,)), ((), ()))
NT = (((1,), (1,)), ((), ()))
TN = (((0,), (0,)), ((), ()))
MESH = pl.DeviceIdType.MESH

K = 2
T, D, F = 1024, 1024, 896
TC = T // K
TR = 64 // K
TO = TC // 8
HALF = TC // 2
DH = D // 2
SEMS = 512
STRIP = 16


def dot(a, b, dims):
    return lax.dot_general(a, b, dims, preferred_element_type=F32)


def power_two(e):
    out = jnp.full(e.shape, 2.0**-10, F32)
    for n in range(-9, -5):
        out = jnp.where(e == n, F32(2.0**n), out)
    return out


def strips(n, body):
    lax.fori_loop(0, n // STRIP, lambda i, c: (body(pl.ds(pl.multiple_of(i * STRIP, STRIP), STRIP)), c)[1], 0)


def kernel(
    xc, xe, gc, ge, uc, ue, dc, de, tgt,
    gx, gg, gu, gd, ego, euo, edo,
    wg, wu, wd, stage, xw, part, sib_b, zs_b, zr_b, own_b, sib_f, zs_f, zr_f, own_f,
    act, gfac, hw, guw, dw,
    d_s, d_r1a, d_r1b, d_s2a, d_s2b, d_r2a, d_r2b,
    h_s, h_r1a, h_r1b, h_s2a, h_s2b, h_r2a, h_r2b,
    ostage, eg_own, eg_sib, eg_z, ed_x, ed_y, sg, su, sd, sgi, sui, sdi, xs,
    ssem, rsem, lsem, osem,
):
    r, c = lax.axis_index("row"), lax.axis_index("col")
    x, y, z, k = r // 4, r % 4, c // 2, c % 2

    def dev(dx=0, dy=0, dz=0, dk=0):
        return (((x + dx) % 4) * 4 + (y + dy) % 4, ((z + dz) % 4) * 2 + (k + dk) % 2)

    used = [0]
    pending = []

    def send(src, dst, to):
        i = used[0]
        used[0] += 1
        cp = pltpu.make_async_remote_copy(
            src_ref=src, dst_ref=dst, send_sem=ssem.at[i], recv_sem=rsem.at[i],
            device_id=to, device_id_type=MESH,
        )
        cp.start()
        pending.append(cp)
        return cp

    def sent(cp):
        cp.wait_send()
        pending[:] = [p for p in pending if p is not cp]

    def fetch(hbm, i, cols):
        return pltpu.make_async_copy(
            hbm.at[pl.ds(i * 128, 128), :], stage.at[i, :, pl.ds(0, cols)], lsem.at[i]
        )

    for i in range(8):
        fetch(gc, i, F).start()

    barrier = pltpu.get_barrier_semaphore()
    peers = [dev(dx=o) for o in (1, 2, 3)] + [dev(dy=o) for o in (1, 2, 3)]
    peers += [dev(dz=o) for o in (1, 2, 3)] + [dev(dk=1)]
    for p in peers:
        pl.semaphore_signal(barrier, inc=1, device_id=p, device_id_type=MESH)

    xs[...] = power_two(xe[...])
    for q in range(K):
        xw[q, x, y] = (xc[q * TR : (q + 1) * TR, :].astype(F32) * xs[...]).astype(BF16)
    pl.semaphore_wait(barrier, len(peers))

    def ag_row1(buf, q):
        a = [send(buf.at[q, x, y, :, pl.ds(0, DH)], buf.at[q, x, y, :, pl.ds(0, DH)], dev(dx=o)) for o in (1, 3, 2)]
        b = [send(buf.at[q, x, y, :, pl.ds(DH, DH)], buf.at[q, x, y, :, pl.ds(DH, DH)], dev(dy=o)) for o in (1, 3, 2)]
        return a, b

    def ag_row2(buf, q, first):
        for cp in first[0]:
            cp.wait_recv()
        a = [send(buf.at[q, :, y, :, pl.ds(0, DH)], buf.at[q, :, y, :, pl.ds(0, DH)], dev(dy=o)) for o in (1, 3, 2)]
        for cp in first[1]:
            cp.wait_recv()
        b = [send(buf.at[q, x, :, :, pl.ds(DH, DH)], buf.at[q, x, :, :, pl.ds(DH, DH)], dev(dx=o)) for o in (1, 3, 2)]
        return a + b

    def arrived(cps):
        for cp in cps:
            cp.wait_recv()

    def rs_row1(s, r1a, r1b, q):
        a = [send(s.at[q, (x + o) % 4, :, :, pl.ds(0, DH)], r1a.at[q, o - 1], dev(dx=o)) for o in (2, 1, 3)]
        b = [send(s.at[q, :, (y + o) % 4, :, pl.ds(DH, DH)], r1b.at[q, o - 1], dev(dy=o)) for o in (2, 1, 3)]
        return a, b

    def rs_row2(s, r1a, r1b, s2a, s2b, r2a, r2b, q, first):
        arrived(first[0])
        for j in range(4):
            v = s[q, x, j, :, 0:DH].astype(F32)
            for o in range(3):
                v += r1a[q, o, j].astype(F32)
            s2a[q, j] = v.astype(BF16)
        a = [send(s2a.at[q, (y + o) % 4], r2a.at[q, o - 1], dev(dy=o)) for o in (2, 1, 3)]
        arrived(first[1])
        for j in range(4):
            v = s[q, j, y, :, DH:D].astype(F32)
            for o in range(3):
                v += r1b[q, o, j].astype(F32)
            s2b[q, j] = v.astype(BF16)
        b = [send(s2b.at[q, (x + o) % 4], r2b.at[q, o - 1], dev(dx=o)) for o in (2, 1, 3)]
        return a, b

    def rs_row3(s2a, s2b, r2a, r2b, q, second):
        arrived(second[0])
        a = s2a[q, y].astype(F32)
        for o in range(3):
            a += r2a[q, o].astype(F32)
        arrived(second[1])
        b = s2b[q, x].astype(F32)
        for o in range(3):
            b += r2b[q, o].astype(F32)
        return a, b

    def rs_sib(slot, dst):
        return send(part.at[slot, pl.ds((1 - k) * HALF, HALF), :], dst, dev(dk=1))

    def rs_z(slot, sib, zs, zr, own, cp):
        cp.wait_recv()
        base = k * HALF

        def add(rows):
            v = part[slot, pl.ds(base + rows.start, STRIP), :] + sib[rows, :]
            zs[rows, :] = v.astype(zs.dtype)

        strips(HALF, add)

        def keep(rows):
            at = z * TO + rows.start
            own[rows, :] = part[slot, pl.ds(base + at, STRIP), :] + sib[pl.ds(at, STRIP), :]

        strips(TO, keep)
        out = [send(zs.at[pl.ds(((z + o) % 4) * TO, TO), :], zr.at[o - 1], dev(dz=o)) for o in (2, 1, 3)]
        sent(cp)
        return out

    def ag_col1(buf, q):
        mine = buf.at[q, k * 4 + z]
        out = [send(mine, mine, dev(dz=o)) for o in (2, 1, 3)]
        return out, send(mine, mine, dev(dk=1))

    def ag_col2(buf, q, first):
        out = [first[1]]
        for o, cp in zip((2, 1, 3), first[0]):
            cp.wait_recv()
            there = buf.at[q, k * 4 + (z + 4 - o) % 4]
            out.append(send(there, there, dev(dk=1)))
        return out

    def convert(hbm, n, dst, cols, nxt, nxt_n, nxt_cols):
        def body(i):
            fetch(hbm, i, cols).wait()
            for h in range(0, 128, 32):
                dst[pl.ds(pl.multiple_of(i * 128 + h, 32), 32), :] = (
                    stage[i, h : h + 32, 0:cols].astype(F32).astype(BF16)
                )

        def step(i, carry):
            body(i)
            if nxt is not None:
                fetch(nxt, i, nxt_cols).start()
            return carry

        both = min(n, nxt_n) if nxt is not None else n
        lax.fori_loop(0, both, step, 0)
        for i in range(both, n):
            body(i)

    def whole(buf, q):
        return buf[q].reshape(TC, buf.shape[-1])

    a1 = [ag_row1(xw, q) for q in range(K)]
    sg[...] = power_two(ge[...])
    su[...] = power_two(ue[...])
    sd[...] = power_two(de[...])
    sgi[...] = 1.0 / sg[...]
    sui[...] = 1.0 / su[...]
    sdi[...] = 1.0 / sd[...]
    convert(gc, 8, wg, F, uc, 8, F)
    a2 = [ag_row2(xw, q, a1[q]) for q in range(K)]
    convert(uc, 8, wu, F, dc, 7, D)

    def matmul_f(slot, lhs, w, dims):
        for j in range(0, F, 256):
            n = min(256, F - j)
            rhs = w[:, j : j + n] if dims is NN else w[j : j + n, :]
            part[slot, :, j : j + n] = dot(lhs(), rhs, dims)

    b_z = []
    for q in range(K):
        arrived(a2[q])
        sibs = []
        for g, w in ((0, wg), (1, wu)):
            matmul_f(g, lambda q=q: whole(xw, q), w, NN)
            sibs.append(rs_sib(g, sib_b.at[q, g]))
        b_z.append([
            rs_z(g, sib_b.at[q, g], zs_b.at[q, g], zr_b.at[q, g], own_b.at[q, g], sibs[g]) for g in (0, 1)
        ])
        if q == 0:
            convert(dc, 7, wd, D, None, 0, 0)

    c1 = []
    for q in range(K):
        arrived(b_z[q][0] + b_z[q][1])

        def silu(rows, q=q):
            def total(g):
                v = own_b[q, g, rows, :]
                for o in range(3):
                    v += zr_b[q, g, o, rows, :].astype(F32)
                return v

            gs = total(0) * sg[...]
            us = total(1) * su[...]
            s = jax.nn.sigmoid(gs)
            a = gs * s
            act[q, rows, :] = a
            gfac[q, rows, :] = us * s * (1.0 + gs * (1.0 - s))
            hw[q, k * 4 + z, rows, :] = (a * us).astype(BF16)

        strips(TO, silu)
        c1.append(ag_col1(hw, q))

    d1 = []
    for q in range(K):
        arrived(ag_col2(hw, q, c1[q]))
        for j in range(0, D, 256):
            v = dot(whole(hw, q), wd[:, j : j + 256], NN).astype(BF16)
            d_s[q, :, :, :, j : j + 256] = v.reshape(4, 4, TR, 256)
        d1.append(rs_row1(d_s, d_r1a, d_r1b, q))
    d2 = [rs_row2(d_s, d_r1a, d_r1b, d_s2a, d_s2b, d_r2a, d_r2b, q, d1[q]) for q in range(K)]

    e1 = []
    for q in range(K):
        a, b = rs_row3(d_s2a, d_s2b, d_r2a, d_r2b, q, d2[q])
        rows = slice(q * TR, (q + 1) * TR)
        for v, cols in ((a, slice(0, DH)), (b, slice(DH, D))):
            delta = (v * sd[:, cols] - tgt[rows, cols].astype(F32)).astype(BF16)
            dw[q, x, y, :, cols] = (delta.astype(F32) * sd[:, cols]).astype(BF16)
        e1.append(ag_row1(dw, q))
    e2 = [ag_row2(dw, q, e1[q]) for q in range(K)]

    f_z = []
    sibs = []
    for q in range(K):
        arrived(e2[q])
        matmul_f(q % 2, lambda q=q: whole(dw, q), wd, NT)
        sibs.append(rs_sib(q % 2, sib_f.at[q]))
        if q % 2 == 1 or q == K - 1:
            for p in range(q - q % 2, q + 1):
                f_z.append(rs_z(p % 2, sib_f.at[p], zs_f.at[p], zr_f.at[p], own_f.at[p], sibs[p]))

    tiles = [0]
    outs = [None, None]

    def weight_grad(lhs, rhs, w, inv, hbm, n, cols):
        acc = jnp.zeros((8, cols), F32)
        for i in range(0, n, 256):
            m = min(256, n - i)
            slot = tiles[0] % 2
            tiles[0] += 1
            if outs[slot] is not None:
                outs[slot].wait()
            ostage[slot, 0:m, 0:cols] = dot(lhs(i, m), rhs(), TN)

            def body(t, acc, i=i, slot=slot):
                rows = pl.ds(pl.multiple_of(t * STRIP, STRIP), STRIP)
                codes = w[pl.ds(pl.multiple_of(i + t * STRIP, STRIP), STRIP), :].astype(F32)
                v = ostage[slot, rows, 0:cols] * inv[...]
                e = v * codes
                ostage[slot, rows, 0:cols] = jnp.where((codes > -8.0) & (codes < 7.0), v, 0.0)
                return acc + (e[0:8] + e[8:16])

            acc = lax.fori_loop(0, m // STRIP, body, acc)
            cp = pltpu.make_async_copy(
                ostage.at[slot, pl.ds(0, m), pl.ds(0, cols)], hbm.at[pl.ds(i, m), :], osem.at[slot]
            )
            cp.start()
            outs[slot] = cp
        return acc

    g1 = []
    for q in range(K):
        arrived(f_z[q])

        def backward(rows, q=q):
            b = own_f[q, rows, :]
            for o in range(3):
                b += zr_f[q, o, rows, :].astype(F32)
            guw[q, k * 4 + z, rows, 0:F] = (b * gfac[q, rows, :] * sg[...]).astype(BF16)
            guw[q, k * 4 + z, rows, F : 2 * F] = (b * act[q, rows, :] * su[...]).astype(BF16)

        strips(TO, backward)
        g1.append(ag_col1(guw, q))

    ed_x[x] = weight_grad(
        lambda i, m: hw[:, :, :, i : i + m].reshape(T, m), lambda: dw[...].reshape(T, D), wd, sdi, gd, F, D
    )
    edx = [send(ed_x.at[x], ed_x.at[x], dev(dx=o)) for o in (1, 3, 2)]

    h1 = []
    for q in range(K):
        arrived(ag_col2(guw, q, g1[q]))
        for j in range(0, D, 256):
            v = dot(guw[q, :, :, 0:F].reshape(TC, F), wg[j : j + 256, :], NT)
            v += dot(guw[q, :, :, F : 2 * F].reshape(TC, F), wu[j : j + 256, :], NT)
            h_s[q, :, :, :, j : j + 256] = v.astype(BF16).reshape(4, 4, TR, 256)
        h1.append(rs_row1(h_s, h_r1a, h_r1b, q))

    arrived(edx)
    ed_y[y] = ed_x[0] + ed_x[1] + ed_x[2] + ed_x[3]
    edy = [send(ed_y.at[y], ed_y.at[y], dev(dy=o)) for o in (1, 3, 2)]

    h2 = [rs_row2(h_s, h_r1a, h_r1b, h_s2a, h_s2b, h_r2a, h_r2b, q, h1[q]) for q in range(K)]

    def x_cols(i, m):
        return xw[:, :, :, :, i : i + m].reshape(T, m)

    eg_own[:, 0:F] = weight_grad(x_cols, lambda: guw[:, :, :, 0:F].reshape(T, F), wg, sgi, gg, D, F)
    eg_own[:, F : 2 * F] = weight_grad(x_cols, lambda: guw[:, :, :, F : 2 * F].reshape(T, F), wu, sui, gu, D, F)
    eg = send(eg_own, eg_sib, dev(dk=1))

    for q in range(K):
        a, b = rs_row3(h_s2a, h_s2b, h_r2a, h_r2b, q, h2[q])
        rows = slice(q * TR, (q + 1) * TR)
        for v, cols in ((a, slice(0, DH)), (b, slice(DH, D))):
            gx[rows, cols] = jnp.where(jnp.abs(xc[rows, cols]) < 127, v, 0.0)

    eg.wait_recv()
    eg_z[z] = eg_own[...] + eg_sib[...]
    egz = [send(eg_z.at[z], eg_z.at[z], dev(dz=o)) for o in (1, 3, 2)]
    arrived(edy)
    ed = ed_y[0] + ed_y[1] + ed_y[2] + ed_y[3]
    edo[...] = LN2 * sd[...] * jnp.sum(ed, axis=0, keepdims=True)
    arrived(egz)
    tot = jnp.sum(eg_z[0] + eg_z[1] + eg_z[2] + eg_z[3], axis=0, keepdims=True)
    ego[...] = LN2 * sg[...] * tot[:, 0:F]
    euo[...] = LN2 * su[...] * tot[:, F : 2 * F]
    for cp in list(pending):
        sent(cp)
    for cp in outs:
        cp.wait()


def per_device(x_codes, x_exp, gate_codes, gate_exp, up_codes, up_exp, down_codes, down_exp, target):
    vm = pl.BlockSpec(memory_space=pltpu.VMEM)
    hbm = pl.BlockSpec(memory_space=pl.ANY)
    V = pltpu.VMEM

    def row_sum_buffers():
        return [
            V((K, 4, 4, TR, D), BF16), V((K, 3, 4, TR, DH), BF16), V((K, 3, 4, TR, DH), BF16),
            V((K, 4, TR, DH), BF16), V((K, 4, TR, DH), BF16),
            V((K, 3, TR, DH), BF16), V((K, 3, TR, DH), BF16),
        ]

    scratch = [
        V((D, F), BF16), V((D, F), BF16), V((F, D), BF16), V((8, 128, D), jnp.int32),
        V((K, 4, 4, TR, D), BF16), V((2, TC, F), F32),
        V((K, 2, HALF, F), F32), V((K, 2, HALF, F), F32), V((K, 2, 3, TO, F), F32), V((K, 2, TO, F), F32),
        V((K, HALF, F), F32), V((K, HALF, F), BF16), V((K, 3, TO, F), BF16), V((K, TO, F), F32),
        V((K, TO, F), F32), V((K, TO, F), F32),
        V((K, 8, TO, F), BF16), V((K, 8, TO, 2 * F), BF16), V((K, 4, 4, TR, D), BF16),
        *row_sum_buffers(), *row_sum_buffers(),
        V((2, 256, D), F32),
        V((8, 2 * F), F32), V((8, 2 * F), F32), V((4, 8, 2 * F), F32), V((4, 8, D), F32), V((4, 8, D), F32),
        V((1, F), F32), V((1, F), F32), V((1, D), F32), V((1, F), F32), V((1, F), F32), V((1, D), F32), V((1, D), F32),
        pltpu.SemaphoreType.DMA((SEMS,)), pltpu.SemaphoreType.DMA((SEMS,)),
        pltpu.SemaphoreType.DMA((8,)), pltpu.SemaphoreType.DMA((2,)),
    ]
    S = jax.ShapeDtypeStruct
    gx, gg, gu, gd, eg, eu, ed = pl.pallas_call(
        kernel,
        out_shape=(
            S((64, D), F32), S((D, F), F32), S((D, F), F32), S((F, D), F32),
            S((1, F), F32), S((1, F), F32), S((1, D), F32),
        ),
        in_specs=[vm, vm, hbm, vm, hbm, vm, hbm, vm, vm],
        out_specs=(vm, hbm, hbm, hbm, vm, vm, vm),
        scratch_shapes=scratch,
        compiler_params=pltpu.CompilerParams(
            collective_id=0, has_side_effects=True, vmem_limit_bytes=62 * 2**20
        ),
        cost_estimate=pl.CostEstimate(flops=18 * 1024 * 1024 * 896, bytes_accessed=24 * 2**20, transcendentals=0),
        name="layer",
    )(
        x_codes, x_exp.reshape(1, D), gate_codes, gate_exp.reshape(1, F), up_codes, up_exp.reshape(1, F),
        down_codes, down_exp.reshape(1, D), target,
    )
    return gx, gg, gu, gd, eg.reshape(F), eu.reshape(F), ed.reshape(D)


def solution(mesh):
    return jax.shard_map(
        per_device,
        mesh=mesh,
        in_specs=(
            P("row", "col"),
            P("col"),
            P("col", "row"),
            P("row"),
            P("col", "row"),
            P("row"),
            P("row", "col"),
            P("col"),
            P("row", "col"),
        ),
        out_specs=(
            P("row", "col"),
            P("col", "row"),
            P("col", "row"),
            P("row", "col"),
            P("row"),
            P("row"),
            P("col"),
        ),
        check_vma=False,
    )
```

```python
import math

import jax
import jax.numpy as jnp
from jax import lax
from jax.experimental import pallas as pl
from jax.experimental.pallas import tpu as pltpu
from jax.sharding import PartitionSpec as P

LN2 = math.log(2.0)
F32, BF16, I16 = jnp.float32, jnp.bfloat16, jnp.int16
NN = (((1,), (0,)), ((), ()))
NT = (((1,), (1,)), ((), ()))
TN = (((0,), (0,)), ((), ()))
MESH = pl.DeviceIdType.MESH

K = 4
T, D, F = 1024, 1024, 896
TC = T // K
TR = 64 // K
TO = TC // 8
HALF = TC // 2
DH = D // 2
SEMS = 512
STRIP = 16
QMAX = 32766.0
ORDER = "".join((
    "01320c1c203100c113201303012123",
    "010103321002321301232123302023",
    "ddd21d03132d2uu0uuuuu2u13ud123",
    "u",
))


def dot(a, b, dims):
    return lax.dot_general(a, b, dims, preferred_element_type=F32)


def power_two(e):
    out = jnp.full(e.shape, 2.0**-10, F32)
    for n in range(-9, -5):
        out = jnp.where(e == n, F32(2.0**n), out)
    return out


def strips(n, body):
    lax.fori_loop(0, n // STRIP, lambda i, c: (body(pl.ds(pl.multiple_of(i * STRIP, STRIP), STRIP)), c)[1], 0)


def kernel(
    xc, xe, gc, ge, uc, ue, dc, de, tgt,
    gx, gg, gu, gd, ego, euo, edo,
    wg, wu, wd, stage, xw, part_b, part_f, sib_b, zs_b, zr_b, zm_s, zm_r, own_b, sib_f, zs_f, zr_f, own_f,
    act, gfac, hw, guw, dw,
    d_s, d_r1a, d_r1b, d_s2a, d_s2b, d_r2a, d_r2b,
    h_s, h_r1a, h_r1b, h_s2a, h_s2b, h_r2a, h_r2b,
    ostage, eg_own, eg_sib, eg_z, ed_x, ed_y, sg, su, sd, sgi, sui, sdi, xs,
    ssem, rsem, lsem, osem,
):
    r, c = lax.axis_index("row"), lax.axis_index("col")
    x, y, z, k = r // 4, r % 4, c // 2, c % 2

    def dev(dx=0, dy=0, dz=0, dk=0):
        return (((x + dx) % 4) * 4 + (y + dy) % 4, ((z + dz) % 4) * 2 + (k + dk) % 2)

    used = [0]
    pending = []

    def send(src, dst, to):
        i = used[0]
        used[0] += 1
        cp = pltpu.make_async_remote_copy(
            src_ref=src, dst_ref=dst, send_sem=ssem.at[i], recv_sem=rsem.at[i],
            device_id=to, device_id_type=MESH,
        )
        cp.start()
        pending.append(cp)
        return cp

    def sent(cp):
        cp.wait_send()
        pending[:] = [p for p in pending if p is not cp]

    def fetch(hbm, i, cols):
        return pltpu.make_async_copy(
            hbm.at[pl.ds(i * 128, 128), :], stage.at[i, :, pl.ds(0, cols)], lsem.at[i]
        )

    for i in range(8):
        fetch(gc, i, F).start()

    barrier = pltpu.get_barrier_semaphore()
    peers = [dev(dx=o) for o in (1, 2, 3)] + [dev(dy=o) for o in (1, 2, 3)]
    peers += [dev(dz=o) for o in (1, 2, 3)] + [dev(dk=1)]
    for p in peers:
        pl.semaphore_signal(barrier, inc=1, device_id=p, device_id_type=MESH)

    xs[...] = power_two(xe[...].reshape(1, D))

    def ag_row1(buf, q):
        a = [send(buf.at[q, x, y, :, pl.ds(0, DH)], buf.at[q, x, y, :, pl.ds(0, DH)], dev(dx=o)) for o in (1, 3, 2)]
        b = [send(buf.at[q, x, y, :, pl.ds(DH, DH)], buf.at[q, x, y, :, pl.ds(DH, DH)], dev(dy=o)) for o in (1, 3, 2)]
        return a, b

    def ag_row2(buf, q, first):
        for cp in first[0]:
            cp.wait_recv()
        a = [send(buf.at[q, :, y, :, pl.ds(0, DH)], buf.at[q, :, y, :, pl.ds(0, DH)], dev(dy=o)) for o in (1, 3, 2)]
        for cp in first[1]:
            cp.wait_recv()
        b = [send(buf.at[q, x, :, :, pl.ds(DH, DH)], buf.at[q, x, :, :, pl.ds(DH, DH)], dev(dx=o)) for o in (1, 3, 2)]
        return a + b

    def arrived(cps):
        for cp in cps:
            cp.wait_recv()

    def rs_row1(s, r1a, r1b, q):
        a = [send(s.at[q, (x + o) % 4, :, :, pl.ds(0, DH)], r1a.at[q, o - 1], dev(dx=o)) for o in (2, 1, 3)]
        b = [send(s.at[q, :, (y + o) % 4, :, pl.ds(DH, DH)], r1b.at[q, o - 1], dev(dy=o)) for o in (2, 1, 3)]
        return a, b

    def rs_row2(s, r1a, r1b, s2a, s2b, r2a, r2b, q, first):
        arrived(first[0])
        for j in range(4):
            v = s[q, x, j, :, 0:DH].astype(F32)
            for o in range(3):
                v += r1a[q, o, j].astype(F32)
            s2a[q, j] = v.astype(BF16)
        a = [send(s2a.at[q, (y + o) % 4], r2a.at[q, o - 1], dev(dy=o)) for o in (2, 1, 3)]
        arrived(first[1])
        for j in range(4):
            v = s[q, j, y, :, DH:D].astype(F32)
            for o in range(3):
                v += r1b[q, o, j].astype(F32)
            s2b[q, j] = v.astype(BF16)
        b = [send(s2b.at[q, (x + o) % 4], r2b.at[q, o - 1], dev(dx=o)) for o in (2, 1, 3)]
        return a, b

    def rs_row3(s2a, s2b, r2a, r2b, q, second):
        arrived(second[0])
        a = s2a[q, y].astype(F32)
        for o in range(3):
            a += r2a[q, o].astype(F32)
        arrived(second[1])
        b = s2b[q, x].astype(F32)
        for o in range(3):
            b += r2b[q, o].astype(F32)
        return a, b

    def rs_sib(src, dst):
        return send(src.at[pl.ds((1 - k) * HALF, HALF), :], dst, dev(dk=1))

    def keep(src, own):
        def copy(rows):
            own[rows, :] = src[pl.ds(k * HALF + z * TO + rows.start, STRIP), :]

        strips(TO, copy)

    def rs_add(src, sib, zs, own, cp):
        cp.wait_recv()

        def add(rows):
            at = pl.ds(k * HALF + rows.start, STRIP)
            v = src[at, :] + sib[rows, :]
            src[at, :] = v
            zs[rows, :] = v.astype(BF16)

        strips(HALF, add)
        keep(src, own)
        sent(cp)

    def spread(tile):
        row = jnp.concatenate([tile] * (F // 128), axis=1)
        return jnp.concatenate([row] * (STRIP // 8), axis=0)

    def rs_code(src, sib, zs, zm, own, cp):
        cp.wait_recv()

        def add(i, most):
            rows = pl.ds(pl.multiple_of(i * STRIP, STRIP), STRIP)
            at = pl.ds(k * HALF + rows.start, STRIP)
            v = src[at, :] + sib[rows, :]
            src[at, :] = v
            v = jnp.abs(v)
            for a in range(0, STRIP, 8):
                for b in range(0, F, 128):
                    most = jnp.maximum(most, v[a : a + 8, b : b + 128])
            return most

        most = lax.fori_loop(0, HALF // STRIP, add, jnp.full((8, 128), 1e-30, F32))
        zm[...] = most
        scale = spread(QMAX / most)

        def code(rows):
            v = src[pl.ds(k * HALF + rows.start, STRIP), :] * scale
            zs[rows, :] = jnp.round(v).astype(jnp.int32).astype(I16)

        strips(HALF, code)
        keep(src, own)
        sent(cp)

    def rs_z(zs, zr):
        return [send(zs.at[pl.ds(((z + o) % 4) * TO, TO), :], zr.at[o - 1], dev(dz=o)) for o in (2, 1, 3)]

    def ag_col1(buf, q):
        mine = buf.at[q, k * 4 + z]
        out = [send(mine, mine, dev(dz=o)) for o in (2, 1, 3)]
        return out, send(mine, mine, dev(dk=1))

    def ag_col2(buf, q, first):
        out = [first[1]]
        for o, cp in zip((2, 1, 3), first[0]):
            cp.wait_recv()
            there = buf.at[q, k * 4 + (z + 4 - o) % 4]
            out.append(send(there, there, dev(dk=1)))
        return out

    def convert(hbm, n, dst, cols, nxt, nxt_n, nxt_cols):
        def body(i):
            fetch(hbm, i, cols).wait()
            for h in range(0, 128, 32):
                dst[pl.ds(pl.multiple_of(i * 128 + h, 32), 32), :] = (
                    stage[i, h : h + 32, 0:cols].astype(F32).astype(BF16)
                )

        def step(i, carry):
            body(i)
            if nxt is not None:
                fetch(nxt, i, nxt_cols).start()
            return carry

        both = min(n, nxt_n) if nxt is not None else n
        lax.fori_loop(0, both, step, 0)
        for i in range(both, n):
            body(i)

    def whole(buf, q):
        return buf[q].reshape(TC, buf.shape[-1])

    def matmul_f(slot, lhs, w, dims):
        for j in range(0, F, 256):
            n = min(256, F - j)
            rhs = w[:, j : j + n] if dims is NN else w[j : j + n, :]
            slot[:, j : j + n] = dot(lhs(), rhs, dims)

    tiles = [0]
    outs = [None, None]

    def weight_grad(lhs, rhs, w, inv, hbm, i, n, cols, acc):
        m = min(256, n - i)
        slot = tiles[0] % 2
        tiles[0] += 1
        if outs[slot] is not None:
            outs[slot].wait()
        ostage[slot, 0:m, 0:cols] = dot(lhs(i, m), rhs(), TN)

        def body(t, total):
            rows = pl.ds(pl.multiple_of(t * STRIP, STRIP), STRIP)
            codes = w[pl.ds(pl.multiple_of(i + t * STRIP, STRIP), STRIP), :].astype(F32)
            v = ostage[slot, rows, 0:cols] * inv[...]
            e = v * codes
            ostage[slot, rows, 0:cols] = jnp.where((codes > -8.0) & (codes < 7.0), v, 0.0)
            return total + (e[0:8] + e[8:16])

        total = lax.fori_loop(0, m // STRIP, body, jnp.zeros((8, cols), F32))
        acc[...] = total if i == 0 else acc[...] + total
        cp = pltpu.make_async_copy(
            ostage.at[slot, pl.ds(0, m), pl.ds(0, cols)], hbm.at[pl.ds(i, m), :], osem.at[slot]
        )
        cp.start()
        outs[slot] = cp

    def chunk(q):
        xw[q, x, y] = (xc[q * TR : (q + 1) * TR, :].astype(F32) * xs[...]).astype(BF16)
        if q == 0:
            pl.semaphore_wait(barrier, len(peers))
        first = ag_row1(xw, q)
        yield
        second = ag_row2(xw, q, first)
        yield
        arrived(second)
        sibs = []
        for g, w in ((0, wg), (1, wu)):
            matmul_f(part_b.at[q % 2, g], lambda: whole(xw, q), w, NN)
            sibs.append(rs_sib(part_b.at[q % 2, g], sib_b.at[q, g]))
        yield
        for g in (0, 1):
            rs_code(part_b.at[q % 2, g], sib_b.at[q, g], zs_b.at[q, g], zm_s.at[q, g], own_b.at[q, g], sibs[g])
        yield
        zcp = [c for g in (0, 1) for c in rs_z(zs_b.at[q, g], zr_b.at[q, g])]
        zcp += [send(zm_s.at[q], zm_r.at[q, o - 1], dev(dz=o)) for o in (2, 1, 3)]
        yield
        arrived(zcp)
        scale = [[spread(zm_r[q, o, g] * (1.0 / QMAX)) for o in range(3)] for g in (0, 1)]

        def silu(rows):
            def total(g):
                v = own_b[q, g, rows, :]
                for o in range(3):
                    v += zr_b[q, g, o, rows, :].astype(jnp.int32).astype(F32) * scale[g][o]
                return v

            gs = total(0) * sg[...]
            us = total(1) * su[...]
            s = jax.nn.sigmoid(gs)
            a = gs * s
            act[q, rows, :] = a
            gfac[q, rows, :] = us * s * (1.0 + gs * (1.0 - s))
            hw[q, k * 4 + z, rows, :] = (a * us).astype(BF16)

        strips(TO, silu)
        first = ag_col1(hw, q)
        yield
        second = ag_col2(hw, q, first)
        yield
        arrived(second)
        for j in range(0, D, 256):
            v = dot(whole(hw, q), wd[:, j : j + 256], NN).astype(BF16)
            d_s[q, :, :, :, j : j + 256] = v.reshape(4, 4, TR, 256)
        first = rs_row1(d_s, d_r1a, d_r1b, q)
        yield
        second = rs_row2(d_s, d_r1a, d_r1b, d_s2a, d_s2b, d_r2a, d_r2b, q, first)
        yield
        a, b = rs_row3(d_s2a, d_s2b, d_r2a, d_r2b, q, second)
        rows = slice(q * TR, (q + 1) * TR)
        for v, cols in ((a, slice(0, DH)), (b, slice(DH, D))):
            delta = (v * sd[:, cols] - tgt[rows, cols].astype(F32)).astype(BF16)
            dw[q, x, y, :, cols] = (delta.astype(F32) * sd[:, cols]).astype(BF16)
        first = ag_row1(dw, q)
        yield
        second = ag_row2(dw, q, first)
        yield
        arrived(second)
        matmul_f(part_f.at[q % 2], lambda: whole(dw, q), wd, NT)
        sib = rs_sib(part_f.at[q % 2], sib_f.at[q])
        yield
        rs_add(part_f.at[q % 2], sib_f.at[q], zs_f.at[q], own_f.at[q], sib)
        zcp = rs_z(zs_f.at[q], zr_f.at[q])
        yield

        def backward(rows):
            b = own_f[q, rows, :]
            for o in range(3):
                b += zr_f[q, o, rows, :].astype(F32)
            guw[q, k * 4 + z, rows, 0:F] = (b * gfac[q, rows, :] * sg[...]).astype(BF16)
            guw[q, k * 4 + z, rows, F : 2 * F] = (b * act[q, rows, :] * su[...]).astype(BF16)

        arrived(zcp)
        strips(TO, backward)
        first = ag_col1(guw, q)
        yield
        second = ag_col2(guw, q, first)
        yield
        arrived(second)
        for j in range(0, D, 256):
            v = dot(guw[q, :, :, 0:F].reshape(TC, F), wg[j : j + 256, :], NT)
            v += dot(guw[q, :, :, F : 2 * F].reshape(TC, F), wu[j : j + 256, :], NT)
            h_s[q, :, :, :, j : j + 256] = v.astype(BF16).reshape(4, 4, TR, 256)
        first = rs_row1(h_s, h_r1a, h_r1b, q)
        yield
        second = rs_row2(h_s, h_r1a, h_r1b, h_s2a, h_s2b, h_r2a, h_r2b, q, first)
        yield
        a, b = rs_row3(h_s2a, h_s2b, h_r2a, h_r2b, q, second)
        rows = slice(q * TR, (q + 1) * TR)
        for v, cols in ((a, slice(0, DH)), (b, slice(DH, D))):
            gx[rows, cols] = jnp.where(jnp.abs(xc[rows, cols]) < 127, v, 0.0)
        yield

    def codes():
        convert(gc, 8, wg, F, uc, 8, F)
        yield
        convert(uc, 8, wu, F, dc, 7, D)
        yield
        convert(dc, 7, wd, D, None, 0, 0)
        yield

    def down_grad():
        for i in range(0, F, 256):
            weight_grad(
                lambda i, m: hw[:, :, :, i : i + m].reshape(T, m), lambda: dw[...].reshape(T, D),
                wd, sdi, gd, i, F, D, ed_x.at[x],
            )
            if i + 256 < F:
                yield
        edx = [send(ed_x.at[x], ed_x.at[x], dev(dx=o)) for o in (1, 3, 2)]
        yield
        arrived(edx)
        ed_y[y] = ed_x[0] + ed_x[1] + ed_x[2] + ed_x[3]
        edy = [send(ed_y.at[y], ed_y.at[y], dev(dy=o)) for o in (1, 3, 2)]
        yield
        arrived(edy)
        ed = ed_y[0] + ed_y[1] + ed_y[2] + ed_y[3]
        edo[...] = LN2 * sd[...] * jnp.sum(ed, axis=0, keepdims=True)
        yield

    def up_grads():
        def x_cols(i, m):
            return xw[:, :, :, :, i : i + m].reshape(T, m)

        for g, w, inv, hbm in ((0, wg, sgi, gg), (1, wu, sui, gu)):
            for i in range(0, D, 256):
                weight_grad(
                    x_cols, lambda: guw[:, :, :, g * F : (g + 1) * F].reshape(T, F),
                    w, inv, hbm, i, D, F, eg_own.at[:, pl.ds(g * F, F)],
                )
                if i + 256 < D or g == 0:
                    yield
        eg = send(eg_own, eg_sib, dev(dk=1))
        yield
        eg.wait_recv()
        eg_z[z] = eg_own[...] + eg_sib[...]
        egz = [send(eg_z.at[z], eg_z.at[z], dev(dz=o)) for o in (1, 3, 2)]
        yield
        arrived(egz)
        tot = jnp.sum(eg_z[0] + eg_z[1] + eg_z[2] + eg_z[3], axis=0, keepdims=True)
        ego[...] = LN2 * sg[...] * tot[:, 0:F]
        euo[...] = LN2 * su[...] * tot[:, F : 2 * F]
        yield

    sg[...] = power_two(ge[...].reshape(1, F))
    su[...] = power_two(ue[...].reshape(1, F))
    sd[...] = power_two(de[...].reshape(1, D))
    sgi[...] = 1.0 / sg[...]
    sui[...] = 1.0 / su[...]
    sdi[...] = 1.0 / sd[...]
    lanes = {str(q): chunk(q) for q in range(K)}
    lanes.update(c=codes(), d=down_grad(), u=up_grads())
    for name in ORDER:
        next(lanes[name])
    for lane in lanes.values():
        if next(lane, None) is not None or lane.gi_frame is not None:
            raise ValueError("steps left")
    for cp in list(pending):
        sent(cp)
    for cp in outs:
        cp.wait()


def results(gx, gg, gu, gd, eg, eu, ed, gxo, ggo, guo, gdo, ego, euo, edo, buf, isem, osem):
    jobs = []
    for n, (a, b) in enumerate(((gg, ggo), (gu, guo), (gd, gdo))):
        rows, cols = a.shape[0] // 4, a.shape[1]
        for i in range(4):
            at = buf.at[n * 4 + i, pl.ds(0, rows), pl.ds(0, cols)]
            s = n * 4 + i
            jobs.append((
                pltpu.make_async_copy(a.at[pl.ds(i * rows, rows), :], at, isem.at[s]),
                pltpu.make_async_copy(at, b.at[pl.ds(i * rows, rows), :], osem.at[s]),
            ))
    for i, _ in jobs:
        i.start()
    gxo[...] = gx[...]
    ego[...] = eg[...].reshape(F)
    euo[...] = eu[...].reshape(F)
    edo[...] = ed[...].reshape(D)
    for i, o in jobs:
        i.wait()
        o.start()
    for _, o in jobs:
        o.wait()


def per_device(x_codes, x_exp, gate_codes, gate_exp, up_codes, up_exp, down_codes, down_exp, target):
    vm = pl.BlockSpec(memory_space=pltpu.VMEM)
    hbm = pl.BlockSpec(memory_space=pl.ANY)
    V = pltpu.VMEM

    def row_sum_buffers():
        return [
            V((K, 4, 4, TR, D), BF16), V((K, 3, 4, TR, DH), BF16), V((K, 3, 4, TR, DH), BF16),
            V((K, 4, TR, DH), BF16), V((K, 4, TR, DH), BF16),
            V((K, 3, TR, DH), BF16), V((K, 3, TR, DH), BF16),
        ]

    scratch = [
        V((D, F), BF16), V((D, F), BF16), V((F, D), BF16), V((8, 128, D), jnp.int32),
        V((K, 4, 4, TR, D), BF16), V((2, 2, TC, F), F32), V((2, TC, F), F32),
        V((K, 2, HALF, F), F32), V((K, 2, HALF, F), I16), V((K, 2, 3, TO, F), I16),
        V((K, 2, 8, 128), F32), V((K, 3, 2, 8, 128), F32), V((K, 2, TO, F), F32),
        V((K, HALF, F), F32), V((K, HALF, F), BF16), V((K, 3, TO, F), BF16), V((K, TO, F), F32),
        V((K, TO, F), F32), V((K, TO, F), F32),
        V((K, 8, TO, F), BF16), V((K, 8, TO, 2 * F), BF16), V((K, 4, 4, TR, D), BF16),
        *row_sum_buffers(), *row_sum_buffers(),
        V((2, 256, D), F32),
        V((8, 2 * F), F32), V((8, 2 * F), F32), V((4, 8, 2 * F), F32), V((4, 8, D), F32), V((4, 8, D), F32),
        V((1, F), F32), V((1, F), F32), V((1, D), F32), V((1, F), F32), V((1, F), F32), V((1, D), F32), V((1, D), F32),
        pltpu.SemaphoreType.DMA((SEMS,)), pltpu.SemaphoreType.DMA((SEMS,)),
        pltpu.SemaphoreType.DMA((8,)), pltpu.SemaphoreType.DMA((2,)),
    ]
    S = jax.ShapeDtypeStruct
    gx, gg, gu, gd, eg, eu, ed = pl.pallas_call(
        kernel,
        out_shape=(
            S((64, D), F32), S((D, F), F32), S((D, F), F32), S((F, D), F32),
            S((1, F), F32), S((1, F), F32), S((1, D), F32),
        ),
        in_specs=[vm, vm, hbm, vm, hbm, vm, hbm, vm, vm],
        out_specs=(vm, hbm, hbm, hbm, vm, vm, vm),
        scratch_shapes=scratch,
        compiler_params=pltpu.CompilerParams(
            collective_id=0, has_side_effects=True, vmem_limit_bytes=62 * 2**20
        ),
        cost_estimate=pl.CostEstimate(flops=18 * 1024 * 1024 * 896, bytes_accessed=24 * 2**20, transcendentals=0),
        name="layer",
    )(
        x_codes, x_exp, gate_codes, gate_exp, up_codes, up_exp, down_codes, down_exp, target,
    )
    return pl.pallas_call(
        results,
        out_shape=(
            S((64, D), F32), S((D, F), F32), S((D, F), F32), S((F, D), F32), S((F,), F32), S((F,), F32), S((D,), F32),
        ),
        in_specs=[vm, hbm, hbm, hbm, vm, vm, vm],
        out_specs=(vm, hbm, hbm, hbm, vm, vm, vm),
        scratch_shapes=[V((12, 256, D), F32), pltpu.SemaphoreType.DMA((12,)), pltpu.SemaphoreType.DMA((12,))],
        compiler_params=pltpu.CompilerParams(vmem_limit_bytes=62 * 2**20),
        cost_estimate=pl.CostEstimate(flops=0, bytes_accessed=24 * 2**20, transcendentals=0),
        name="results",
    )(gx, gg, gu, gd, eg, eu, ed)


def solution(mesh):
    return jax.shard_map(
        per_device,
        mesh=mesh,
        in_specs=(
            P("row", "col"),
            P("col"),
            P("col", "row"),
            P("row"),
            P("col", "row"),
            P("row"),
            P("row", "col"),
            P("col"),
            P("row", "col"),
        ),
        out_specs=(
            P("row", "col"),
            P("col", "row"),
            P("col", "row"),
            P("row", "col"),
            P("row"),
            P("row"),
            P("col"),
        ),
        check_vma=False,
    )
```
